32 devices in a mesh: groups: 2 (over y), req: 4 (over z), head: 2 (over x), sub: 2 (over core).
Axes of the slice: x: 2, y: 2, z: 4, core: 2. Of those that a mesh axis runs over, the one named last changes fastest.
Arguments:
- hidden_in: bfloat16 [1024, 8192], P(('groups', 'req')), parts along dimension 0, may hold values from -3 to 3
- q_weight: bfloat16 [8192, 8192], P('req', ('head', 'sub')), may hold values from -0.0625 to 0.0625
- q_gain: float32 [128], replicated, may hold values from 0.1 to 1.9
- key_cache: bfloat16 [8, 1601, 1024], P(('groups', 'req'), None, 'head'), parts along dimension 0, may hold values from -64 to 64
- value_cache: bfloat16 [8, 1601, 1024], P(('groups', 'req'), None, 'head'), parts along dimension 0, may hold values from -8 to 8
- out_weight: bfloat16 [8192, 8192], P(('head', 'sub'), 'req'), may hold values from -0.09375 to 0.09375
- req_image: int32 [1024], P(('groups', 'req')), parts along dimension 0, may hold values from 0 to 3, as said below
- image_count: int32 [1024], P(('groups', 'req')), parts along dimension 0, may hold values from 0 to 1, as said below
- image_home: int32 [8], P('groups'), parts along dimension 0, may hold values from 0 to 3, as said below
Outputs:
- layer_out: bfloat16 [1024, 8192], P(('groups', 'req'), ('head', 'sub')), parts along dimension 0
The draws below stay inside these ranges and needn't reach their ends.
There are 2 independent parts, one for each index of `groups`. The reference program is written for one: setup_inputs(seed, part) draws one part's arguments, and reference() takes and returns one part's arrays. A program takes and returns all parts, laid end to end along the dimension named above; an argument that names none is the same for every part. Nothing has to cross between parts.
Inputs may be any that keep to these rules, and one draw needn't show every extreme that they name: Requests with image_count 0 attend to nothing; in each aligned block of 128 requests at most a quarter have image_count 0. In each aligned block of 128 requests, at most 64 requests with image_count 1 have one and the same value of image_home[req_image]; in every block exactly 64 of them share one value, and that value is the same for all blocks. `image_home`: each cache row holds exactly one image.
All inputs are finite; a program needn't handle non-finite values.
Results may differ from the reference program's by a relative error of at most 0.025.
Values may be sent and summed in bfloat16 or wider, within the bound.
A program may use at most 128 MiB of HBM per device.

```python
import jax
import jax.numpy as jnp
from jax import lax

D = 8192
HQ = 64
KVH = 8
HD = 128
TOK = 1601
R_DEV = 128
REQS = 512
IMAGES = 4
CAP = 64
N_REQ = 4
N_HEAD = 2
N_SUB = 2


def routing_tables(key):
    base_key = jax.random.fold_in(key, 29)
    key_hot, key_blocks = jax.random.split(base_key, 2)
    key_home = jax.random.fold_in(jax.random.fold_in(key, 97), 5)
    image_home = jax.random.permutation(key_home, IMAGES).astype(jnp.int32)
    image_at_row = jnp.zeros((IMAGES,), jnp.int32).at[image_home].set(jnp.arange(IMAGES, dtype=jnp.int32))
    hottest = jax.random.randint(key_hot, (), 0, IMAGES).astype(jnp.int32)
    others = (hottest + 1 + jnp.arange(IMAGES - 1, dtype=jnp.int32)) % IMAGES
    spread = jnp.repeat(others, CAP)

    def one_block(block_key):
        key_perm, key_skip, key_order, key_free = jax.random.split(block_key, 4)
        tickets = jnp.concatenate([jnp.zeros((CAP,), jnp.int32) + hottest, jax.random.permutation(key_perm, spread)])
        skipped = jax.random.randint(key_skip, (), 0, R_DEV // 4 + 1).astype(jnp.int32)
        visit_order = jax.random.permutation(key_order, R_DEV).astype(jnp.int32)
        rank_of = jnp.zeros((R_DEV,), jnp.int32).at[visit_order].set(jnp.arange(R_DEV, dtype=jnp.int32))
        counts = (rank_of >= skipped).astype(jnp.int32)
        ticket_index = jnp.clip(rank_of - skipped, 0, tickets.shape[0] - 1)
        home_pick = tickets[ticket_index]
        unused_image = jax.random.randint(key_free, (R_DEV,), 0, IMAGES).astype(jnp.int32)
        chosen_image = jnp.where(counts == 1, image_at_row[home_pick], unused_image)
        return (chosen_image, counts)
    block_keys = jax.random.split(key_blocks, IMAGES)
    images, counts = jax.vmap(one_block)(block_keys)
    return (images.reshape(-1).astype(jnp.int32), counts.reshape(-1).astype(jnp.int32), image_home)


def draw_req_image(key, part):
    return routing_tables(key)[0]


def draw_image_count(key, part):
    return routing_tables(key)[1]


def draw_image_home(key, part):
    return routing_tables(key)[2]


def draw_key_cache(key, part):
    cache_shape = (IMAGES, TOK, KVH * HD)
    drawn = jnp.clip(2.0 * jax.random.normal(jax.random.fold_in(key, 4), cache_shape, jnp.float32), -8.0, 8.0)
    return drawn.astype(jnp.bfloat16)


def with_spikes(entries, key, source, target, blocks, factor):
    def block_of(position):
        return (jnp.arange(entries.shape[position]) // (entries.shape[position] // blocks)).reshape((-1,) + (1,) * (entries.ndim - 1 - position))

    near = jax.random.permutation(key, blocks)[block_of(target)]
    far = (block_of(target) + blocks // 2) % blocks
    return jnp.where((block_of(source) == near) | (block_of(source) == far), factor * entries, entries)


def shard_levels(key, dims, pieces, low, largest):
    def one(dim, blocks):
        draws = jax.random.uniform(jax.random.fold_in(jax.random.fold_in(key, 6), dim), (blocks,), jnp.float32, low / len(pieces), largest / len(pieces))
        return jnp.repeat(jnp.exp(draws), dims[dim] // blocks).reshape((-1,) + (1,) * (len(dims) - dim - 1))

    level = one(*pieces[0])
    for cut in pieces[1:]:
        level = level * one(*cut)
    return level


def centred(own_key, dims, deviation, reach, cuts=(), kind=jnp.bfloat16):
    factor_of = shard_levels(own_key, dims, cuts, -0.22, 0.18) if cuts else 1.0
    entries = jax.random.normal(own_key, dims, jnp.float32) * deviation * factor_of
    return jnp.minimum(jnp.maximum(entries, -reach), reach).astype(kind)


def bell_draw_with(stream_key, shape, width, most, shards, heavy, kind=jnp.bfloat16):
    result = width * jax.random.normal(stream_key, shape, jnp.float32)
    if shards:
        result = result * shard_levels(stream_key, shape, shards, -0.22, 0.18)
    return jnp.clip(with_spikes(result, jax.random.fold_in(stream_key, 3), *heavy), -most, most).astype(kind)


def setup_inputs(seed: int = 0, part: int = 0) -> dict:
    seeds = jax.random.split(jax.random.key(seed), 10)
    part_keys = jax.random.split(jax.random.fold_in(seeds[9], part), 10)
    return {
        "hidden_in": centred(part_keys[0], (REQS, D), 0.5, 3.0, ((0, 4),)),
        "q_weight": centred(seeds[1], (D, HQ * HD), D ** -0.5, 0.0625, ((0, 4), (1, 4))),
        "q_gain": jnp.clip(1.0 + 0.18 * jax.random.normal(seeds[2], (HD,), jnp.float32), 0.1, 1.9),
        "key_cache": draw_key_cache(jax.random.fold_in(jax.random.fold_in(seeds[9], part), 71), part),
        "value_cache": centred(part_keys[4], (IMAGES, TOK, KVH * HD), 2.0, 8.0, ((0, 4), (2, 2))),
        "out_weight": bell_draw_with(seeds[5], (HQ * HD, D), (HQ * HD) ** -0.5, 0.09375, ((0, 4), (1, 4)), (0, 1, 4, 2.0)),
        "req_image": draw_req_image(jax.random.fold_in(jax.random.fold_in(seeds[9], part), 71), part),
        "image_count": draw_image_count(jax.random.fold_in(jax.random.fold_in(seeds[9], part), 71), part),
        "image_home": draw_image_home(jax.random.fold_in(jax.random.fold_in(seeds[9], part), 71), part),
    }


def normalize_heads(queries, q_gain, head_dim):
    row_count = queries.shape[0]
    per_head = queries.astype(jnp.float32).reshape(row_count, -1, head_dim)
    inv_rms = lax.rsqrt(lax.optimization_barrier(jnp.mean(per_head * per_head, axis=2, keepdims=True)) + 1e-05)
    return (per_head * inv_rms * q_gain).reshape(row_count, -1).astype(jnp.bfloat16)

def reference(hidden_in, q_weight, q_gain, key_cache, value_cache, out_weight, req_image, image_count, image_home):
    row_total = hidden_in.shape[0]
    feat_block = D // N_REQ
    q_width = HQ * HD

    def add_block(running, block_index):
        column_part = lax.dynamic_slice_in_dim(hidden_in, block_index * feat_block, feat_block, 1)
        weight_part = lax.dynamic_slice_in_dim(q_weight, block_index * feat_block, feat_block, 0)
        partial_value = lax.optimization_barrier(jnp.dot(column_part, weight_part, preferred_element_type=jnp.float32).astype(jnp.bfloat16))
        return (running + partial_value.astype(jnp.float32), None)
    query_sum, _ = lax.scan(add_block, jnp.zeros((row_total, q_width), jnp.float32), jnp.arange(N_REQ, dtype=jnp.int32))
    queries = lax.optimization_barrier(query_sum.astype(jnp.bfloat16))
    normalized = normalize_heads(queries, q_gain, HD)
    home_row = image_home[req_image].astype(jnp.int32)
    group_size = HQ // KVH
    request_block = 8

    def attend_block(block_args):
        rows_here, queries_here, counts_here = block_args
        key_rows = key_cache[rows_here].astype(jnp.float32).reshape(request_block, TOK, KVH, HD)
        value_rows = value_cache[rows_here].astype(jnp.float32).reshape(request_block, TOK, KVH, HD)
        query_part = queries_here.astype(jnp.float32).reshape(request_block, KVH, group_size, HD)
        scores = jnp.einsum('bkgd,btkd->bkgt', query_part, key_rows) * HD ** (-0.5)
        scores = scores - lax.optimization_barrier(jnp.max(scores, axis=3, keepdims=True))
        weights = jnp.exp(scores)
        probs = (weights / lax.optimization_barrier(jnp.sum(weights, axis=3, keepdims=True))).astype(jnp.bfloat16)
        mixed_heads = jnp.einsum('bkgt,btkd->bkgd', probs.astype(jnp.float32), value_rows)
        mixed_heads = mixed_heads.astype(jnp.bfloat16).reshape(request_block, q_width)
        return jnp.where(counts_here[:, None] == 1, mixed_heads, jnp.zeros_like(mixed_heads))
    attended = lax.map(attend_block, (home_row.reshape(-1, request_block), normalized.reshape(-1, request_block, q_width), image_count.reshape(-1, request_block)))
    attended = attended.reshape(row_total, q_width)
    group_cols = q_width // (N_HEAD * N_SUB)

    def add_group(running, group_index):
        column_part = lax.dynamic_slice_in_dim(attended, group_index * group_cols, group_cols, 1)
        weight_part = lax.dynamic_slice_in_dim(out_weight, group_index * group_cols, group_cols, 0)
        partial_value = lax.optimization_barrier(jnp.dot(column_part, weight_part, preferred_element_type=jnp.float32).astype(jnp.bfloat16))
        return (running + partial_value.astype(jnp.float32), None)
    head_total, _ = lax.scan(add_group, jnp.zeros((row_total, D), jnp.float32), jnp.arange(N_HEAD * N_SUB, dtype=jnp.int32))
    return (hidden_in.astype(jnp.float32) + head_total).astype(jnp.bfloat16)
```

```python
import jax
import jax.numpy as jnp
from jax import lax
from jax.sharding import PartitionSpec as P

HQ = 64
KVH = 8


def normalize_heads(queries, q_gain, head_dim):
    row_count = queries.shape[0]
    per_head = queries.astype(jnp.float32).reshape(row_count, -1, head_dim)
    inv_rms = lax.rsqrt(jnp.mean(per_head * per_head, axis=2, keepdims=True) + 1e-05)
    return (per_head * inv_rms * q_gain).reshape(row_count, -1).astype(jnp.bfloat16)


def local(
    hidden_in,
    q_weight,
    q_gain,
    key_cache,
    value_cache,
    out_weight,
    req_image,
    image_count,
    image_home,
):
    req_count = lax.axis_size("req")
    local_rows = hidden_in.shape[0]
    q_cols = q_weight.shape[1]
    head_dim = q_gain.shape[0]
    group_size = HQ // KVH
    heads_here = q_cols // head_dim
    sub_count = lax.axis_size("sub")
    part = q_weight.shape[0] // sub_count
    mine = lax.dynamic_index_in_dim(
        hidden_in.reshape(local_rows, req_count, sub_count, part),
        lax.axis_index("sub"),
        2,
        keepdims=False,
    )
    mine = mine.transpose(1, 0, 2)
    spread = lax.all_to_all(mine, "req", split_axis=0, concat_axis=0, tiled=True)
    spread = lax.all_gather(spread.reshape(-1, part), "sub", axis=0, tiled=False)
    query_part = jnp.einsum(
        "kmi,kin->mn",
        spread,
        q_weight.reshape(sub_count, part, q_cols),
        preferred_element_type=jnp.float32,
    )
    query_sum = lax.psum_scatter(
        query_part.astype(jnp.bfloat16),
        "req",
        scatter_dimension=0,
        tiled=True,
    )
    queries = lax.optimization_barrier(query_sum)
    normalized = normalize_heads(queries, q_gain, head_dim)
    capacity = 2 * local_rows // req_count
    slot_total = req_count * capacity
    table_ids = lax.broadcasted_iota(jnp.int32, (local_rows, image_home.shape[0]), 1)
    home_rows = jnp.sum(jnp.where(req_image[:, None] == table_ids, image_home[None, :], 0), axis=1)
    wanted = image_count == 1
    dest_ids = lax.broadcasted_iota(jnp.int32, (local_rows, req_count), 1)
    to_dest = ((home_rows[:, None] == dest_ids) & wanted[:, None]).astype(jnp.int32)
    earlier = jnp.cumsum(to_dest, axis=0) - to_dest
    position = home_rows * capacity + jnp.sum(earlier * to_dest, axis=1)
    slot_ids = lax.broadcasted_iota(jnp.int32, (slot_total, local_rows), 0)
    dispatch = ((slot_ids == position[None, :]) & wanted[None, :]).astype(jnp.bfloat16)
    outgoing = jnp.dot(dispatch, normalized, preferred_element_type=jnp.float32).astype(
        jnp.bfloat16
    )
    outgoing = outgoing.reshape(req_count, capacity, q_cols)
    kv_count = max(1, heads_here // group_size)
    per_kv = heads_here // kv_count
    sub_index = lax.axis_index("sub")
    kv_first = sub_index * heads_here // group_size
    keys_here = lax.dynamic_slice_in_dim(
        key_cache[0], kv_first * head_dim, kv_count * head_dim, 1
    ).reshape(-1, kv_count, head_dim)
    values_here = lax.dynamic_slice_in_dim(
        value_cache[0], kv_first * head_dim, kv_count * head_dim, 1
    ).reshape(-1, kv_count, head_dim)
    score_scale = head_dim ** (-0.5)
    arrived = lax.all_to_all(outgoing, "req", split_axis=0, concat_axis=0, tiled=True)
    sources = arrived.shape[0]
    slot_count = arrived.shape[1]
    flat_rows = arrived.reshape(sources * slot_count, kv_count, per_kv, head_dim)
    scores = (
        jnp.einsum("mkgd,tkd->kgmt", flat_rows, keys_here, preferred_element_type=jnp.float32)
        * score_scale
    )
    row_peak = jnp.max(scores, axis=3, keepdims=True)
    weights = jnp.exp(scores - row_peak)
    probs = (weights / jnp.sum(weights, axis=3, keepdims=True)).astype(jnp.bfloat16)
    mixed_heads = jnp.einsum(
        "kgmt,tkd->mkgd", probs, values_here, preferred_element_type=jnp.float32
    )
    replies = mixed_heads.astype(jnp.bfloat16).reshape(sources, slot_count, q_cols)
    returned = lax.all_to_all(replies, "req", split_axis=0, concat_axis=0, tiled=True)
    attended = lax.dot_general(
        dispatch,
        returned.reshape(slot_total, q_cols),
        (((0,), (0,)), ((), ())),
        preferred_element_type=jnp.float32,
    ).astype(jnp.bfloat16)
    partial_cols = jnp.dot(
        lax.all_gather(attended, "req", axis=0, tiled=True),
        out_weight,
        preferred_element_type=jnp.float32,
    )
    head_sum = lax.psum_scatter(
        partial_cols.astype(jnp.bfloat16), ("head", "sub"), scatter_dimension=1, tiled=True
    )
    piece = head_sum.shape[1]
    by_owner = lax.all_to_all(
        head_sum.reshape(req_count, local_rows, piece), "req", split_axis=0, concat_axis=0, tiled=True
    )
    lanes = lax.axis_size("head") * sub_count
    blocks = lax.all_to_all(by_owner, ("head", "sub"), split_axis=0, concat_axis=0, tiled=True)
    blocks = blocks.reshape(lanes, req_count // lanes, local_rows, piece)
    head_total = blocks.transpose(2, 1, 0, 3).reshape(local_rows, -1).astype(jnp.float32)
    out_width = head_total.shape[1]
    column_index = lax.axis_index("head") * lax.axis_size("sub") + lax.axis_index("sub")
    residual = lax.dynamic_slice_in_dim(hidden_in, column_index * out_width, out_width, 1)
    return (residual.astype(jnp.float32) + head_total).astype(jnp.bfloat16)


def solution(mesh):
    in_specs = (
        P(("groups", "req"), None),
        P("req", ("head", "sub")),
        P(),
        P(("groups", "req"), None, "head"),
        P(("groups", "req"), None, "head"),
        P(("head", "sub"), "req"),
        P(("groups", "req")),
        P(("groups", "req")),
        P("groups"),
    )
    out_specs = P(("groups", "req"), ("head", "sub"))
    return jax.shard_map(local, mesh=mesh, in_specs=in_specs, out_specs=out_specs, check_vma=False)
```

```python
import functools

import jax
import jax.numpy as jnp
from jax import lax
from jax.experimental import pallas as pl
from jax.experimental.pallas import tpu as pltpu
from jax.sharding import PartitionSpec as P

HQ = 64
KVH = 8


def normalize_heads(queries, q_gain, head_dim):
    row_count = queries.shape[0]
    per_head = queries.astype(jnp.float32).reshape(row_count, -1, head_dim)
    inv_rms = lax.rsqrt(jnp.mean(per_head * per_head, axis=2, keepdims=True) + 1e-05)
    return (per_head * inv_rms * q_gain).reshape(row_count, -1).astype(jnp.bfloat16)


MESH = pl.DeviceIdType.MESH


def out_kernel(
    n,
    lanes,
    n_sub,
    tile,
    att_ref,
    w_hbm,
    res_ref,
    out_ref,
    w_v,
    gath,
    part,
    rs,
    fin,
    land,
    w_sem,
    r_send,
    l_send,
    g_recv,
    rs_send,
    rs_recv,
    f_send,
    f_recv,
):
    g, r = lax.axis_index("groups"), lax.axis_index("req")
    me = lax.axis_index("head") * n_sub + lax.axis_index("sub")
    rows = att_ref.shape[0] // lanes
    has_left, has_right = r > 0, r < n - 1
    on_self = r == me

    def dev(row, lane):
        return (g, row, lax.div(lane, n_sub), lax.rem(lane, n_sub))

    load = pltpu.make_async_copy(w_hbm, w_v, w_sem)
    load.start()

    barrier = pltpu.get_barrier_semaphore()

    def greet(row, lane):
        pl.semaphore_signal(barrier, inc=1, device_id=dev(row, lane), device_id_type=MESH)

    pl.when(has_left)(lambda: greet(r - 1, me))
    pl.when(has_right)(lambda: greet(r + 1, me))
    for d in range(1, lanes):
        greet(r, lax.rem(me + d, lanes))
    for q in range(lanes):
        pl.when(jnp.logical_not(on_self & (me == q)))(functools.partial(greet, me, jnp.int32(q)))
    neighbours = jnp.where(has_left, 1, 0) + jnp.where(has_right, 1, 0)
    pl.semaphore_wait(barrier, neighbours + (lanes - 1) + n - jnp.where(on_self, 1, 0))

    def block_copy(src, ref, to_right):
        return pltpu.make_async_remote_copy(
            src_ref=ref,
            dst_ref=gath.at[src],
            send_sem=(r_send if to_right else l_send).at[src],
            recv_sem=g_recv.at[src],
            device_id=dev(r + 1 if to_right else r - 1, me),
            device_id_type=MESH,
        )

    def part_copy(src, d):
        lane = lax.rem(me + d, lanes)
        return pltpu.make_async_remote_copy(
            src_ref=part.at[src, lane],
            dst_ref=rs.at[src, d],
            send_sem=rs_send.at[src, d],
            recv_sem=rs_recv.at[src, d],
            device_id=dev(r, lane),
            device_id_type=MESH,
        )

    def owner_copy(src):
        return pltpu.make_async_remote_copy(
            src_ref=fin.at[src],
            dst_ref=land.at[me],
            send_sem=f_send.at[src],
            recv_sem=f_recv.at[me],
            device_id=dev(src, r),
            device_id_type=MESH,
        )

    def process(src, ref):
        @pl.loop(0, w_v.shape[1] // tile)
        def _(c):
            cols = pl.ds(pl.multiple_of(c * tile, tile), tile)
            product = jnp.dot(ref[...], w_v[:, cols], preferred_element_type=jnp.float32)
            part[src, :, :, cols] = product.astype(jnp.bfloat16).reshape(lanes, rows, tile)

        for d in range(1, lanes):
            part_copy(src, d).start()

    def finish(src):
        total = part[src, me].astype(jnp.float32)
        for d in range(1, lanes):
            part_copy(src, d).wait_recv()
            total += rs[src, d].astype(jnp.float32)
        fin[src] = total.astype(jnp.bfloat16)
        local_owner = on_self & (src == r)

        @pl.when(local_owner)
        def _():
            land[me] = fin[src]

        @pl.when(jnp.logical_not(local_owner))
        def _():
            owner_copy(src).start()

    def finish_step(k):
        if k == 0:
            finish(r)
        else:
            pl.when(r >= k)(lambda: finish(r - k))
            pl.when(r + k < n)(lambda: finish(r + k))

    pl.when(has_right)(lambda: block_copy(r, att_ref, True).start())
    pl.when(has_left)(lambda: block_copy(r, att_ref, False).start())
    load.wait()
    process(r, att_ref)
    for k in range(1, n):

        @pl.when(r >= k)
        def _():
            src = r - k
            block_copy(src, gath.at[src], False).wait_recv()
            pl.when(has_right)(lambda: block_copy(src, gath.at[src], True).start())
            process(src, gath.at[src])

        @pl.when(r + k < n)
        def _():
            src = r + k
            block_copy(src, gath.at[src], True).wait_recv()
            pl.when(has_left)(lambda: block_copy(src, gath.at[src], False).start())
            process(src, gath.at[src])

        finish_step(k - 1)
    finish_step(n - 1)

    for q in range(lanes):

        @pl.when(jnp.logical_not(on_self & (me == q)))
        def _():
            pltpu.make_async_remote_copy(
                src_ref=fin.at[0],
                dst_ref=land.at[q],
                send_sem=f_send.at[0],
                recv_sem=f_recv.at[q],
                device_id=dev(me, jnp.int32(q)),
                device_id_type=MESH,
            ).wait_recv()

        here = pl.ds(q * rows, rows)
        out_ref[here, :] = (
            res_ref[here, :].astype(jnp.float32) + land[q].astype(jnp.float32)
        ).astype(jnp.bfloat16)

    pl.when(has_right)(lambda: block_copy(r, att_ref, True).wait_send())
    pl.when(has_left)(lambda: block_copy(r, att_ref, False).wait_send())
    for k in range(1, n):
        pl.when((r >= k) & has_right)(
            lambda: block_copy(r - k, gath.at[r - k], True).wait_send()
        )
        pl.when((r + k < n) & has_left)(
            lambda: block_copy(r + k, gath.at[r + k], False).wait_send()
        )
    for src in range(n):
        for d in range(1, lanes):
            part_copy(src, d).wait_send()
        pl.when(jnp.logical_not(on_self & (r == src)))(
            lambda: owner_copy(jnp.int32(src)).wait_send()
        )


def project_out(attended, out_weight, residual, n, lanes, n_sub):
    local_rows, depth = attended.shape
    width = out_weight.shape[1]
    rows = local_rows // lanes
    vmem = pl.BlockSpec(memory_space=pltpu.VMEM)
    dma = pltpu.SemaphoreType.DMA
    return pl.pallas_call(
        functools.partial(out_kernel, n, lanes, n_sub, min(width, 512)),
        out_shape=jax.ShapeDtypeStruct((local_rows, width), jnp.bfloat16),
        in_specs=[vmem, pl.BlockSpec(memory_space=pl.ANY), vmem],
        out_specs=vmem,
        scratch_shapes=[
            pltpu.VMEM((depth, width), jnp.bfloat16),
            pltpu.VMEM((n, local_rows, depth), jnp.bfloat16),
            pltpu.VMEM((n, lanes, rows, width), jnp.bfloat16),
            pltpu.VMEM((n, lanes, rows, width), jnp.bfloat16),
            pltpu.VMEM((n, rows, width), jnp.bfloat16),
            pltpu.VMEM((lanes, rows, width), jnp.bfloat16),
            dma,
            dma((n,)),
            dma((n,)),
            dma((n,)),
            dma((n, lanes)),
            dma((n, lanes)),
            dma((n,)),
            dma((lanes,)),
        ],
        compiler_params=pltpu.CompilerParams(
            collective_id=0, has_side_effects=True, vmem_limit_bytes=40 * 1024 * 1024
        ),
    )(attended, out_weight, residual)


def local(
    hidden_in,
    q_weight,
    q_gain,
    key_cache,
    value_cache,
    out_weight,
    req_image,
    image_count,
    image_home,
):
    req_count = lax.axis_size("req")
    local_rows = hidden_in.shape[0]
    q_cols = q_weight.shape[1]
    head_dim = q_gain.shape[0]
    group_size = HQ // KVH
    heads_here = q_cols // head_dim
    sub_count = lax.axis_size("sub")
    part = q_weight.shape[0] // sub_count
    mine = lax.dynamic_index_in_dim(
        hidden_in.reshape(local_rows, req_count, sub_count, part),
        lax.axis_index("sub"),
        2,
        keepdims=False,
    )
    mine = mine.transpose(1, 0, 2)
    spread = lax.all_to_all(mine, "req", split_axis=0, concat_axis=0, tiled=True)
    spread = lax.all_gather(spread.reshape(-1, part), "sub", axis=0, tiled=False)
    query_part = jnp.einsum(
        "kmi,kin->mn",
        spread,
        q_weight.reshape(sub_count, part, q_cols),
        preferred_element_type=jnp.float32,
    )
    query_sum = lax.psum_scatter(
        query_part.astype(jnp.bfloat16),
        "req",
        scatter_dimension=0,
        tiled=True,
    )
    queries = lax.optimization_barrier(query_sum)
    normalized = normalize_heads(queries, q_gain, head_dim)
    capacity = 2 * local_rows // req_count
    slot_total = req_count * capacity
    table_ids = lax.broadcasted_iota(jnp.int32, (local_rows, image_home.shape[0]), 1)
    home_rows = jnp.sum(jnp.where(req_image[:, None] == table_ids, image_home[None, :], 0), axis=1)
    wanted = image_count == 1
    dest_ids = lax.broadcasted_iota(jnp.int32, (local_rows, req_count), 1)
    to_dest = ((home_rows[:, None] == dest_ids) & wanted[:, None]).astype(jnp.int32)
    earlier = jnp.cumsum(to_dest, axis=0) - to_dest
    position = home_rows * capacity + jnp.sum(earlier * to_dest, axis=1)
    slot_ids = lax.broadcasted_iota(jnp.int32, (slot_total, local_rows), 0)
    dispatch = ((slot_ids == position[None, :]) & wanted[None, :]).astype(jnp.bfloat16)
    outgoing = jnp.dot(dispatch, normalized, preferred_element_type=jnp.float32).astype(
        jnp.bfloat16
    )
    outgoing = outgoing.reshape(req_count, capacity, q_cols)
    kv_count = max(1, heads_here // group_size)
    per_kv = heads_here // kv_count
    sub_index = lax.axis_index("sub")
    kv_first = sub_index * heads_here // group_size
    keys_here = lax.dynamic_slice_in_dim(
        key_cache[0], kv_first * head_dim, kv_count * head_dim, 1
    ).reshape(-1, kv_count, head_dim)
    values_here = lax.dynamic_slice_in_dim(
        value_cache[0], kv_first * head_dim, kv_count * head_dim, 1
    ).reshape(-1, kv_count, head_dim)
    score_scale = head_dim ** (-0.5)
    arrived = lax.all_to_all(outgoing, "req", split_axis=0, concat_axis=0, tiled=True)
    sources = arrived.shape[0]
    slot_count = arrived.shape[1]
    flat_rows = arrived.reshape(sources * slot_count, kv_count, per_kv, head_dim)
    scores = (
        jnp.einsum("mkgd,tkd->kgmt", flat_rows, keys_here, preferred_element_type=jnp.float32)
        * score_scale
    )
    row_peak = jnp.max(scores, axis=3, keepdims=True)
    weights = jnp.exp(scores - row_peak)
    probs = (weights / jnp.sum(weights, axis=3, keepdims=True)).astype(jnp.bfloat16)
    mixed_heads = jnp.einsum(
        "kgmt,tkd->mkgd", probs, values_here, preferred_element_type=jnp.float32
    )
    replies = mixed_heads.astype(jnp.bfloat16).reshape(sources, slot_count, q_cols)
    returned = lax.all_to_all(replies, "req", split_axis=0, concat_axis=0, tiled=True)
    attended = lax.dot_general(
        dispatch,
        returned.reshape(slot_total, q_cols),
        (((0,), (0,)), ((), ())),
        preferred_element_type=jnp.float32,
    ).astype(jnp.bfloat16)
    lanes = lax.axis_size("head") * sub_count
    column_index = lax.axis_index("head") * sub_count + lax.axis_index("sub")
    if req_count == lanes and local_rows % (16 * lanes) == 0:
        width = out_weight.shape[1]
        residual = lax.dynamic_slice_in_dim(hidden_in, column_index * width, width, 1)
        return project_out(attended, out_weight, residual, req_count, lanes, sub_count)
    partial_cols = jnp.dot(
        lax.all_gather(attended, "req", axis=0, tiled=True),
        out_weight,
        preferred_element_type=jnp.float32,
    )
    head_sum = lax.psum_scatter(
        partial_cols.astype(jnp.bfloat16), ("head", "sub"), scatter_dimension=1, tiled=True
    )
    piece = head_sum.shape[1]
    by_owner = lax.all_to_all(
        head_sum.reshape(req_count, local_rows, piece), "req", split_axis=0, concat_axis=0, tiled=True
    )
    blocks = lax.all_to_all(by_owner, ("head", "sub"), split_axis=0, concat_axis=0, tiled=True)
    blocks = blocks.reshape(lanes, req_count // lanes, local_rows, piece)
    head_total = blocks.transpose(2, 1, 0, 3).reshape(local_rows, -1).astype(jnp.float32)
    out_width = head_total.shape[1]
    residual = lax.dynamic_slice_in_dim(hidden_in, column_index * out_width, out_width, 1)
    return (residual.astype(jnp.float32) + head_total).astype(jnp.bfloat16)


def solution(mesh):
    in_specs = (
        P(("groups", "req"), None),
        P("req", ("head", "sub")),
        P(),
        P(("groups", "req"), None, "head"),
        P(("groups", "req"), None, "head"),
        P(("head", "sub"), "req"),
        P(("groups", "req")),
        P(("groups", "req")),
        P("groups"),
    )
    out_specs = P(("groups", "req"), ("head", "sub"))
    return jax.shard_map(local, mesh=mesh, in_specs=in_specs, out_specs=out_specs, check_vma=False)
```
